32 devices in a mesh: ctx: 16 (over z, y, core), help: 2 (over x).
Axes of the slice: x: 2, y: 2, z: 4, core: 2. Of those that a mesh axis runs over, the one named last changes fastest.
Arguments:
- queries: bfloat16 [2304, 2048], P('ctx', 'help'), may hold values from -18 to 18
- keys: bfloat16 [2304, 2048], P('ctx', 'help'), may hold values from -18 to 18
- values: bfloat16 [2304, 2048], P('ctx', 'help'), may hold values from -6 to 6
- block_pos: int32 [16], replicated, may hold values from 0 to 15, each once
- w_out: bfloat16 [2048, 2048], P('help'), may hold values from -0.125 to 0.125
Outputs:
- mixed: bfloat16 [2304, 2048], P(('ctx', 'help'))
The draws below stay inside these ranges and needn't reach their ends.
Inputs may be any that keep to these rules, and one draw needn't show every extreme that they name: `block_pos`: a permutation: each block place occurs once.
All inputs are finite; a program needn't handle non-finite values.
Results may differ from the reference program's by a relative error of at most 0.009.
Values may be sent and summed in bfloat16 or wider, within the bound.
A program may use at most 64 MiB of HBM per device.

```python
import jax
import jax.numpy as jnp
from jax import lax

HEADS = 16
HEAD_DIM = 128
D = 2048
TOK_DEV = 144
TOKENS = 2304
N_CTX = 16


def draw_queries(key, part):
    key = jax.random.fold_in(key, 1)
    return jnp.clip(jax.random.normal(key, (TOKENS, HEADS * HEAD_DIM), jnp.float32), -6.0, 6.0).astype(jnp.bfloat16)


def draw_keys(key, part):
    key = jax.random.fold_in(key, 2)
    return jnp.clip(jax.random.normal(key, (TOKENS, HEADS * HEAD_DIM), jnp.float32), -6.0, 6.0).astype(jnp.bfloat16)


def level_of(key, dims, cuts, smallest, high):
    def one(axis_at, blocks):
        draws = jax.random.uniform(jax.random.fold_in(jax.random.fold_in(key, 6), axis_at), (blocks,), jnp.float32, smallest / len(cuts), high / len(cuts))
        return jnp.repeat(jnp.exp(draws), dims[axis_at] // blocks).reshape((-1,) + (1,) * (len(dims) - axis_at - 1))

    level = one(*cuts[0])
    for cut in cuts[1:]:
        level = level * one(*cut)
    return level


def bell_draw(own_key, dims, scale, bound, cuts=(), kind=jnp.bfloat16):
    array = scale * jax.random.normal(own_key, dims, jnp.float32)
    if cuts:
        array = array * level_of(own_key, dims, cuts, -0.22, 0.18)
    return jnp.clip(array, -bound, bound).astype(kind)


def setup_inputs(seed: int = 0) -> dict:
    streams_of = jax.random.split(jax.random.key(seed), 6)
    return {
        "queries": draw_queries(jax.random.fold_in(streams_of[5], 71), 0),
        "keys": draw_keys(jax.random.fold_in(streams_of[5], 71), 0),
        "values": bell_draw(streams_of[2], (TOKENS, D), 1.0, 6.0, ((0, 16), (1, 2))),
        "block_pos": jax.random.permutation(streams_of[3], N_CTX).astype(jnp.int32),
        "w_out": bell_draw(streams_of[4], (D, D), D ** -0.5, 0.125, ((0, 2),)),
    }


def reference(queries, keys, values, block_pos, w_out):
    tokens = queries.shape[0]
    width = queries.shape[1]
    offsets = jnp.arange(TOK_DEV, dtype=jnp.int32)
    position = (block_pos[:, None] * TOK_DEV + offsets[None, :]).reshape(tokens).astype(jnp.int32)
    keys_all = keys.astype(jnp.float32).reshape(tokens, HEADS, HEAD_DIM)
    values_all = values.astype(jnp.float32).reshape(tokens, HEADS, HEAD_DIM)
    scale = 1.0 / (HEAD_DIM ** 0.5)

    def one_block(block):
        start = (block * TOK_DEV).astype(jnp.int32)
        rows_q = lax.dynamic_slice_in_dim(queries, start, TOK_DEV, 0).astype(jnp.float32)
        rows_q = rows_q.reshape(TOK_DEV, HEADS, HEAD_DIM)
        rows_pos = lax.dynamic_slice_in_dim(position, start, TOK_DEV, 0)
        scores = jnp.einsum("qhd,khd->hqk", rows_q, keys_all) * scale
        visible = position[None, None, :] <= rows_pos[None, :, None]
        top = jnp.max(jnp.where(visible, scores, -1e30), axis=2)
        weights = jnp.where(visible, jnp.exp(scores - top[:, :, None]), 0.0)
        total = jnp.sum(weights, axis=2)
        probs = weights.astype(jnp.bfloat16).astype(jnp.float32)
        summed = jnp.einsum("hqk,khd->hqd", probs, values_all)
        result = summed / total[:, :, None]
        return jnp.transpose(result, (1, 0, 2)).reshape(TOK_DEV, width).astype(jnp.bfloat16)

    attended = lax.map(one_block, jnp.arange(N_CTX, dtype=jnp.int32)).reshape(tokens, width)
    return jnp.dot(attended, w_out, preferred_element_type=jnp.float32).astype(jnp.bfloat16)
```

```python
import functools
import math

import jax
import jax.numpy as jnp
from jax import lax
from jax.experimental import pallas as pl
from jax.experimental.pallas import tpu as pltpu
from jax.sharding import PartitionSpec as P

HEAD_DIM = 128
MESH = pl.DeviceIdType.MESH


def gathered_body(queries, keys, values, block_pos, w_out):
    n_ctx = lax.axis_size("ctx")
    device = lax.axis_index("ctx")
    rows, width = queries.shape
    heads = width // HEAD_DIM
    scale = 1.0 / HEAD_DIM**0.5
    own_block = jnp.sum(jnp.where(jnp.arange(n_ctx) == device, block_pos, 0))
    query_pos = own_block * rows + jnp.arange(rows, dtype=jnp.int32)
    whole_keys = lax.all_gather(keys, "ctx", axis=0, tiled=True)
    whole_values = lax.all_gather(values, "ctx", axis=0, tiled=True)
    count = whole_keys.shape[0]
    key_pos = (block_pos[:, None] * rows + jnp.arange(rows, dtype=jnp.int32)[None, :]).reshape(count)
    query_heads = queries.reshape(rows, heads, HEAD_DIM)
    key_heads = whole_keys.reshape(count, heads, HEAD_DIM)
    value_heads = whole_values.reshape(count, heads, HEAD_DIM)
    scores = (
        jnp.einsum("qhd,khd->hqk", query_heads, key_heads, preferred_element_type=jnp.float32)
        * scale
    )
    visible = key_pos[None, None, :] <= query_pos[None, :, None]
    top = jnp.max(jnp.where(visible, scores, -1e30), axis=2)
    weights = jnp.where(visible, jnp.exp(scores - top[:, :, None]), 0.0)
    total = jnp.sum(weights, axis=2)
    summed = jnp.einsum(
        "hqk,khd->hqd",
        weights.astype(jnp.bfloat16),
        value_heads,
        preferred_element_type=jnp.float32,
    )
    result = summed / total[:, :, None]
    attended = jnp.transpose(result, (1, 0, 2)).reshape(rows, width).astype(jnp.bfloat16)
    return lax.psum_scatter(
        jnp.dot(attended, w_out, preferred_element_type=jnp.float32).astype(jnp.bfloat16),
        "help",
        scatter_dimension=0,
        tiled=True,
    )


def kernel(
    chips, rows, lanes, parts,
    bp_ref, q_hbm, k_hbm, v_hbm, w_hbm, out_ref,
    qbuf, kv, acc, top, total, qpos, osend, att, wbuf, part, psend, precv,
    own_sem, w_sem, q_send, q_recv, kv_send, kv_recv, relay_send, relay_recv,
    o_own, o_send, o_recv, p_send, p_recv,
):
    ctx = lax.axis_index("ctx")
    helper = lax.axis_index("help")
    chip = lax.div(ctx, 2)
    core = lax.rem(ctx, 2)
    sibling = chip * 2 + (1 - core)
    count = chips * rows
    fold = math.log2(math.e) / HEAD_DIM**0.5

    def peer(step):
        return lax.rem(chip + step, chips)

    def head_of(ref, which):
        return ref.at[:, pl.ds(pl.multiple_of(which * HEAD_DIM, HEAD_DIM), HEAD_DIM)]

    def row_block(ref, which):
        return ref.at[pl.ds(pl.multiple_of(which * rows, 16), rows), :]

    w_copy = pltpu.make_async_copy(w_hbm, wbuf, w_sem)
    own = [
        pltpu.make_async_copy(head_of(q_hbm, chip), row_block(qbuf, chip), own_sem.at[0]),
        pltpu.make_async_copy(head_of(k_hbm, chip), kv.at[chip, core, 0], own_sem.at[1]),
        pltpu.make_async_copy(head_of(v_hbm, chip), kv.at[chip, core, 1], own_sem.at[2]),
    ]
    for copy in own:
        copy.start()

    barrier = pltpu.get_barrier_semaphore()
    for step in range(1, chips):
        pl.semaphore_signal(
            barrier, inc=1, device_id=(peer(step) * 2 + core, helper), device_id_type=MESH
        )
    pl.semaphore_signal(barrier, inc=1, device_id=(sibling, helper), device_id_type=MESH)
    pl.semaphore_signal(barrier, inc=1, device_id=(ctx, 1 - helper), device_id_type=MESH)
    pl.semaphore_wait(barrier, chips + 1)

    def q_copy(step, source):
        return pltpu.make_async_remote_copy(
            src_ref=head_of(q_hbm, peer(step)),
            dst_ref=row_block(qbuf, source),
            send_sem=q_send.at[step],
            recv_sem=q_recv.at[source],
            device_id=(peer(step) * 2 + core, helper),
            device_id_type=MESH,
        )

    def kv_copy(step, source, which):
        return pltpu.make_async_remote_copy(
            src_ref=head_of((k_hbm, v_hbm)[which], peer(step)),
            dst_ref=kv.at[source, core, which],
            send_sem=kv_send.at[step, which],
            recv_sem=kv_recv.at[source, which],
            device_id=(peer(step) * 2 + core, helper),
            device_id_type=MESH,
        )

    def relay(source, half):
        return pltpu.make_async_remote_copy(
            src_ref=kv.at[source, half],
            dst_ref=kv.at[source, half],
            send_sem=relay_send.at[source],
            recv_sem=relay_recv.at[source],
            device_id=(sibling, helper),
            device_id_type=MESH,
        )

    for step in range(1, chips):
        q_copy(step, chip).start()
    for step in range(1, chips):
        kv_copy(step, chip, 0).start()
        kv_copy(step, chip, 1).start()
    w_copy.start()

    lane = lax.broadcasted_iota(jnp.int32, (1, count), 1)
    position = jnp.zeros((1, count), jnp.int32)
    for block in range(chips):
        inside = (lane >= block * rows) & (lane < (block + 1) * rows)
        position = jnp.where(
            inside, lane + (bp_ref[block * 2 + core] - block) * rows, position
        )
    qpos[...] = position
    acc[...] = jnp.zeros_like(acc)
    total[...] = jnp.zeros_like(total)
    top[...] = jnp.full(top.shape, -1e9, jnp.float32)

    def attend(source):
        keys = kv[source, :, 0].reshape(2 * rows, HEAD_DIM)
        values = kv[source, :, 1].reshape(2 * rows, HEAD_DIM).T
        first = bp_ref[source * 2] * rows
        second = bp_ref[source * 2 + 1] * rows
        for begin in range(0, count, lanes):
            cols = pl.ds(begin, lanes)
            raw = lax.dot_general(
                keys, qbuf[cols, :], (((1,), (1,)), ((), ())), preferred_element_type=jnp.float32
            )
            inner = lax.broadcasted_iota(jnp.int32, (rows, lanes), 0)
            place = qpos[:, cols]
            raw = jnp.concatenate(
                [
                    jnp.where(inner <= place - first, raw[:rows], -1e30),
                    jnp.where(inner <= place - second, raw[rows:], -1e30),
                ],
                axis=0,
            )
            before = top[:, cols]
            after = jnp.maximum(before, jnp.max(raw, axis=0, keepdims=True))
            weights = jnp.exp2(raw * fold - after * fold)
            keep = jnp.exp2((before - after) * fold)
            top[:, cols] = after
            total[:, cols] = total[:, cols] * keep + jnp.sum(weights, axis=0, keepdims=True)
            acc[:, cols] = acc[:, cols] * keep + jnp.dot(
                values, weights.astype(jnp.bfloat16), preferred_element_type=jnp.float32
            )

    own[1].wait()
    own[2].wait()
    relay(chip, core).start()
    own[0].wait()
    for step in range(1, chips):
        q_copy(step, peer(step)).wait_recv()

    def one_step(step, carry):
        source = peer(step)
        kv_copy(step, source, 0).wait_recv()
        kv_copy(step, source, 1).wait_recv()
        relay(source, core).start()
        done = peer(step - 1)
        relay(done, 1 - core).wait_recv()
        attend(done)
        return carry

    lax.fori_loop(1, chips, one_step, 0)
    last = peer(chips - 1)
    relay(last, 1 - core).wait_recv()
    attend(last)

    def o_copy(block, head):
        return pltpu.make_async_remote_copy(
            src_ref=osend.at[pl.ds(block * rows, rows), :],
            dst_ref=head_of(att, head),
            send_sem=o_send.at[block],
            recv_sem=o_recv.at[head],
            device_id=(block * 2 + core, helper),
            device_id_type=MESH,
        )

    def o_local(block):
        return pltpu.make_async_copy(
            osend.at[pl.ds(block * rows, rows), :], head_of(att, chip), o_own
        )

    sent = 0
    for begin in range(0, count, lanes):
        cols = pl.ds(begin, lanes)
        result = acc[:, cols] * (1.0 / total[:, cols])
        osend[cols, :] = result.T.astype(jnp.bfloat16)
        while (sent + 1) * rows <= begin + lanes:
            block = sent

            @pl.when(chip == block)
            def _():
                o_local(block).start()

            @pl.when(chip != block)
            def _():
                o_copy(block, chip).start()

            sent += 1

    w_copy.wait()
    for block in range(chips):

        @pl.when(chip == block)
        def _():
            o_local(block).wait()

        @pl.when(chip != block)
        def _():
            o_copy(block, block).wait_recv()

    half = rows // 2
    wide = w_hbm.shape[1] // parts

    def p_copy(index):
        return pltpu.make_async_remote_copy(
            src_ref=psend.at[index],
            dst_ref=precv.at[index],
            send_sem=p_send.at[index],
            recv_sem=p_recv.at[index],
            device_id=(ctx, 1 - helper),
            device_id_type=MESH,
        )

    for index in range(parts):
        cols = pl.ds(index * wide, wide)
        part[:, cols] = jnp.dot(att[...], wbuf[:, cols], preferred_element_type=jnp.float32)
        other = part[pl.ds(pl.multiple_of((1 - helper) * half, 8), half), cols]
        fill = jnp.zeros((psend.shape[1] - half, wide), jnp.float32)
        psend[index] = jnp.concatenate([other, fill], axis=0).astype(jnp.bfloat16)
        p_copy(index).start()
    for index in range(parts):
        cols = pl.ds(index * wide, wide)
        p_copy(index).wait_recv()
        mine = part[pl.ds(pl.multiple_of(helper * half, 8), half), cols]
        out_ref[:, cols] = (mine + precv[index].astype(jnp.float32)[:half]).astype(jnp.bfloat16)

    for step in range(1, chips):
        q_copy(step, chip).wait_send()
        kv_copy(step, chip, 0).wait_send()
        kv_copy(step, chip, 1).wait_send()
    for source in range(chips):
        relay(source, core).wait_send()

        @pl.when(chip != source)
        def _():
            o_copy(source, chip).wait_send()

    for index in range(parts):
        p_copy(index).wait_send()


def exchanged_body(chips, queries, keys, values, block_pos, w_out):
    rows, width = queries.shape
    out_width = w_out.shape[1]
    count = chips * rows
    lanes = 384
    parts = 4
    padded = -(-(rows // 2) // 16) * 16
    bf16, f32 = jnp.bfloat16, jnp.float32
    dma = pltpu.SemaphoreType.DMA
    anywhere = pl.BlockSpec(memory_space=pl.ANY)
    return pl.pallas_call(
        functools.partial(kernel, chips, rows, lanes, parts),
        out_shape=jax.ShapeDtypeStruct((rows // 2, out_width), bf16),
        in_specs=[pl.BlockSpec(memory_space=pltpu.SMEM)] + [anywhere] * 4,
        out_specs=pl.BlockSpec(memory_space=pltpu.VMEM),
        scratch_shapes=[
            pltpu.VMEM((count, HEAD_DIM), bf16),
            pltpu.VMEM((chips, 2, 2, rows, HEAD_DIM), bf16),
            pltpu.VMEM((HEAD_DIM, count), f32),
            pltpu.VMEM((1, count), f32),
            pltpu.VMEM((1, count), f32),
            pltpu.VMEM((1, count), jnp.int32),
            pltpu.VMEM((count, HEAD_DIM), bf16),
            pltpu.VMEM((rows, width), bf16),
            pltpu.VMEM((width, out_width), bf16),
            pltpu.VMEM((rows, out_width), f32),
            pltpu.VMEM((parts, padded, out_width // parts), bf16),
            pltpu.VMEM((parts, padded, out_width // parts), bf16),
            dma((3,)),
            dma,
            dma((chips,)),
            dma((chips,)),
            dma((chips, 2)),
            dma((chips, 2)),
            dma((chips,)),
            dma((chips,)),
            dma,
            dma((chips,)),
            dma((chips,)),
            dma((parts,)),
            dma((parts,)),
        ],
        compiler_params=pltpu.CompilerParams(
            collective_id=0, has_side_effects=True, vmem_limit_bytes=40 * 1024 * 1024
        ),
        cost_estimate=pl.CostEstimate(
            flops=8 * count * count * HEAD_DIM + 2 * rows * width * out_width,
            bytes_accessed=2 * (3 * rows * width + width * out_width),
            transcendentals=2 * count * count,
        ),
        name="exchange_attend_project",
    )(block_pos, queries, keys, values, w_out)


def solution(mesh):
    chips = mesh.shape["ctx"] // 2

    def body(queries, keys, values, block_pos, w_out):
        if mesh.shape["help"] == 2 and queries.shape[1] == chips * HEAD_DIM:
            return exchanged_body(chips, queries, keys, values, block_pos, w_out)
        return gathered_body(queries, keys, values, block_pos, w_out)

    in_specs = (P("ctx", "help"), P("ctx", "help"), P("ctx", "help"), P(), P("help", None))
    out_specs = P(("ctx", "help"), None)
    return jax.shard_map(body, mesh=mesh, in_specs=in_specs, out_specs=out_specs, check_vma=False)
```

```python
import functools
import math

import jax
import jax.numpy as jnp
from jax import lax
from jax.experimental import pallas as pl
from jax.experimental.pallas import tpu as pltpu
from jax.sharding import PartitionSpec as P

HEAD_DIM = 128
MESH = pl.DeviceIdType.MESH


def gathered_body(queries, keys, values, block_pos, w_out):
    n_ctx = lax.axis_size("ctx")
    device = lax.axis_index("ctx")
    rows, width = queries.shape
    heads = width // HEAD_DIM
    scale = 1.0 / HEAD_DIM**0.5
    own_block = jnp.sum(jnp.where(jnp.arange(n_ctx) == device, block_pos, 0))
    query_pos = own_block * rows + jnp.arange(rows, dtype=jnp.int32)
    whole_keys = lax.all_gather(keys, "ctx", axis=0, tiled=True)
    whole_values = lax.all_gather(values, "ctx", axis=0, tiled=True)
    count = whole_keys.shape[0]
    key_pos = (block_pos[:, None] * rows + jnp.arange(rows, dtype=jnp.int32)[None, :]).reshape(count)
    query_heads = queries.reshape(rows, heads, HEAD_DIM)
    key_heads = whole_keys.reshape(count, heads, HEAD_DIM)
    value_heads = whole_values.reshape(count, heads, HEAD_DIM)
    scores = (
        jnp.einsum("qhd,khd->hqk", query_heads, key_heads, preferred_element_type=jnp.float32)
        * scale
    )
    visible = key_pos[None, None, :] <= query_pos[None, :, None]
    top = jnp.max(jnp.where(visible, scores, -1e30), axis=2)
    weights = jnp.where(visible, jnp.exp(scores - top[:, :, None]), 0.0)
    total = jnp.sum(weights, axis=2)
    summed = jnp.einsum(
        "hqk,khd->hqd",
        weights.astype(jnp.bfloat16),
        value_heads,
        preferred_element_type=jnp.float32,
    )
    result = summed / total[:, :, None]
    attended = jnp.transpose(result, (1, 0, 2)).reshape(rows, width).astype(jnp.bfloat16)
    return lax.psum_scatter(
        jnp.dot(attended, w_out, preferred_element_type=jnp.float32).astype(jnp.bfloat16),
        "help",
        scatter_dimension=0,
        tiled=True,
    )


def column_spans(base, width):
    spans = []
    while width:
        lanes = width if width <= 384 else 256
        spans.append((base, lanes))
        base, width = base + lanes, width - lanes
    return tuple(spans)


def kernel(
    chips, rows, parts,
    bp_ref, q_hbm, k_hbm, v_hbm, w_hbm, out_ref,
    qbuf, kv, acc, top, total, qpos, osend, att_a, att_b, wbuf, part, psend, precv,
    own_sem, w_sem, q_send, q_recv, kv_send, kv_recv, relay_send, relay_recv,
    o_own, o_send, o_recv, p_send, p_recv,
):
    ctx = lax.axis_index("ctx")
    helper = lax.axis_index("help")
    chip = lax.div(ctx, 2)
    core = lax.rem(ctx, 2)
    sibling = chip * 2 + (1 - core)
    half = rows // 2
    size = (att_a.shape[0], att_b.shape[0])
    start = ((1 - helper) * size[1], helper * size[0])
    base = (0, chips * size[0])
    spans = tuple(column_spans(base[i], chips * size[i]) for i in range(2))
    att = (att_a, att_b)
    fold = math.log2(math.e) / HEAD_DIM**0.5

    def peer(step):
        found = 0
        for bit in range(chips.bit_length() - 1):
            mine = lax.rem(lax.div(chip, 1 << bit), 2)
            other = step // (1 << bit) % 2 if isinstance(step, int) else lax.rem(
                lax.div(step, 1 << bit), 2
            )
            found = found + (mine + other - 2 * mine * other) * (1 << bit)
        return found

    def head_of(ref, which):
        return ref.at[:, pl.ds(pl.multiple_of(which * HEAD_DIM, HEAD_DIM), HEAD_DIM)]

    def query_rows(which, head):
        return q_hbm.at[
            pl.ds(pl.multiple_of(start[which], 16), size[which]),
            pl.ds(pl.multiple_of(head * HEAD_DIM, HEAD_DIM), HEAD_DIM),
        ]

    def held_rows(ref, which, block):
        return ref.at[pl.ds(pl.multiple_of(base[which] + block * size[which], 16), size[which]), :]

    w_copy = pltpu.make_async_copy(w_hbm, wbuf, w_sem)
    own = [
        pltpu.make_async_copy(head_of(k_hbm, chip), kv.at[chip, core, 0], own_sem.at[0]),
        pltpu.make_async_copy(head_of(v_hbm, chip), kv.at[chip, core, 1], own_sem.at[1]),
        pltpu.make_async_copy(query_rows(0, chip), held_rows(qbuf, 0, chip), own_sem.at[2]),
        pltpu.make_async_copy(query_rows(1, chip), held_rows(qbuf, 1, chip), own_sem.at[3]),
    ]
    for copy in own:
        copy.start()

    barrier = pltpu.get_barrier_semaphore()
    for step in range(1, chips):
        pl.semaphore_signal(
            barrier, inc=1, device_id=(peer(step) * 2 + core, helper), device_id_type=MESH
        )
    pl.semaphore_signal(barrier, inc=1, device_id=(sibling, helper), device_id_type=MESH)
    pl.semaphore_signal(barrier, inc=1, device_id=(ctx, 1 - helper), device_id_type=MESH)
    pl.semaphore_wait(barrier, chips + 1)

    def q_copy(which, step, source):
        return pltpu.make_async_remote_copy(
            src_ref=query_rows(which, peer(step)),
            dst_ref=held_rows(qbuf, which, source),
            send_sem=q_send.at[which, step],
            recv_sem=q_recv.at[which, source],
            device_id=(peer(step) * 2 + core, helper),
            device_id_type=MESH,
        )

    def kv_copy(step, source, which):
        return pltpu.make_async_remote_copy(
            src_ref=head_of((k_hbm, v_hbm)[which], peer(step)),
            dst_ref=kv.at[source, core, which],
            send_sem=kv_send.at[step, which],
            recv_sem=kv_recv.at[source, which],
            device_id=(peer(step) * 2 + core, helper),
            device_id_type=MESH,
        )

    def relay(source, from_core):
        return pltpu.make_async_remote_copy(
            src_ref=kv.at[source, from_core],
            dst_ref=kv.at[source, from_core],
            send_sem=relay_send.at[source],
            recv_sem=relay_recv.at[source],
            device_id=(sibling, helper),
            device_id_type=MESH,
        )

    for step in range(1, chips):
        q_copy(0, step, chip).start()
    for step in range(1, chips):
        kv_copy(step, chip, 0).start()
        kv_copy(step, chip, 1).start()
    for step in range(1, chips):
        q_copy(1, step, chip).start()
    w_copy.start()

    lane = lax.broadcasted_iota(jnp.int32, qpos.shape, 1)
    position = jnp.zeros(qpos.shape, jnp.int32)
    for which in range(2):
        for block in range(chips):
            begin = base[which] + block * size[which]
            inside = (lane >= begin) & (lane < begin + size[which])
            place = bp_ref[block * 2 + core] * rows + start[which] - begin
            position = jnp.where(inside, lane + place, position)
    qpos[...] = position
    acc[...] = jnp.zeros_like(acc)
    total[...] = jnp.zeros_like(total)
    top[...] = jnp.full(top.shape, -1e9, jnp.float32)

    def attend(source, which):
        keys = kv[source, :, 0].reshape(2 * rows, HEAD_DIM)
        values = kv[source, :, 1].reshape(2 * rows, HEAD_DIM).T
        first = bp_ref[source * 2] * rows
        second = bp_ref[source * 2 + 1] * rows
        for begin, lanes in spans[which]:
            cols = pl.ds(begin, lanes)
            raw = lax.dot_general(
                keys, qbuf[cols, :], (((1,), (1,)), ((), ())), preferred_element_type=jnp.float32
            )
            inner = lax.broadcasted_iota(jnp.int32, (rows, lanes), 0)
            place = qpos[:, cols]
            raw = jnp.concatenate(
                [
                    jnp.where(inner <= place - first, raw[:rows], -1e30),
                    jnp.where(inner <= place - second, raw[rows:], -1e30),
                ],
                axis=0,
            )
            before = top[:, cols]
            after = jnp.maximum(before, jnp.max(raw, axis=0, keepdims=True))
            weights = jnp.exp2(raw * fold - after * fold)
            keep = jnp.exp2((before - after) * fold)
            top[:, cols] = after
            total[:, cols] = total[:, cols] * keep + jnp.sum(weights, axis=0, keepdims=True)
            acc[:, cols] = acc[:, cols] * keep + jnp.dot(
                values, weights.astype(jnp.bfloat16), preferred_element_type=jnp.float32
            )

    own[0].wait()
    own[1].wait()
    relay(chip, core).start()
    own[2].wait()
    for step in range(1, chips):
        q_copy(0, step, peer(step)).wait_recv()

    def turn(index):
        return index

    def one_step(index, carry):
        step = turn(index)
        source = peer(step)
        kv_copy(step, source, 0).wait_recv()
        kv_copy(step, source, 1).wait_recv()
        relay(source, core).start()
        done = lax.select(index == 1, chip, peer(turn(index - 1)))
        relay(done, 1 - core).wait_recv()
        attend(done, 0)
        return carry

    lax.fori_loop(1, chips, one_step, 0)
    last = peer(turn(chips - 1))
    relay(last, 1 - core).wait_recv()
    attend(last, 0)

    def o_copy(which, step, head):
        return pltpu.make_async_remote_copy(
            src_ref=held_rows(osend, which, peer(step)),
            dst_ref=head_of(att[which], head),
            send_sem=o_send.at[which, step],
            recv_sem=o_recv.at[which, head],
            device_id=(peer(step) * 2 + core, helper),
            device_id_type=MESH,
        )

    def o_local(which):
        return pltpu.make_async_copy(
            held_rows(osend, which, chip), head_of(att[which], chip), o_own.at[which]
        )

    def give(which):
        for begin, lanes in spans[which]:
            cols = pl.ds(begin, lanes)
            result = acc[:, cols] * (1.0 / total[:, cols])
            osend[cols, :] = result.T.astype(jnp.bfloat16)
        for step in range(1, chips):
            o_copy(which, step, chip).start()
        o_local(which).start()

    def take(which):
        o_local(which).wait()
        for step in range(1, chips):
            o_copy(which, step, peer(step)).wait_recv()

    give(0)
    own[3].wait()
    for step in range(1, chips):
        q_copy(1, step, peer(step)).wait_recv()

    def second_pass(source, carry):
        attend(source, 1)
        return carry

    lax.fori_loop(0, chips, second_pass, 0)
    give(1)

    wide = w_hbm.shape[1] // parts

    def p_copy(index):
        return pltpu.make_async_remote_copy(
            src_ref=psend.at[index],
            dst_ref=precv.at[index],
            send_sem=p_send.at[index],
            recv_sem=p_recv.at[index],
            device_id=(ctx, 1 - helper),
            device_id_type=MESH,
        )

    w_copy.wait()
    take(0)
    for index in range(parts):
        cols = pl.ds(index * wide, wide)
        product = jnp.dot(att_a[...], wbuf[:, cols], preferred_element_type=jnp.float32)
        part[:, cols] = product
        psend[index] = product.astype(jnp.bfloat16)
        p_copy(index).start()
    take(1)
    spare = size[0] - half
    for index in range(parts):
        cols = pl.ds(index * wide, wide)
        product = jnp.dot(att_b[...], wbuf[:, cols], preferred_element_type=jnp.float32)
        mine = jnp.where(
            helper == 0,
            jnp.concatenate([product, part[:spare, cols]], axis=0),
            jnp.concatenate([part[half:, cols], product], axis=0),
        )
        p_copy(index).wait_recv()
        theirs = precv[index].astype(jnp.float32)
        theirs = jnp.where(helper == 0, theirs[:half], theirs[spare:])
        out_ref[:, cols] = (mine + theirs).astype(jnp.bfloat16)

    for step in range(1, chips):
        for which in range(2):
            q_copy(which, step, chip).wait_send()
            kv_copy(step, chip, which).wait_send()
            o_copy(which, step, chip).wait_send()
    for source in range(chips):
        relay(source, core).wait_send()
    for index in range(parts):
        p_copy(index).wait_send()


def exchanged_body(chips, queries, keys, values, block_pos, w_out):
    rows, width = queries.shape
    out_width = w_out.shape[1]
    count = chips * rows
    parts = 4
    first = -(-(rows // 2) // 16) * 16
    bf16, f32 = jnp.bfloat16, jnp.float32
    dma = pltpu.SemaphoreType.DMA
    anywhere = pl.BlockSpec(memory_space=pltpu.HBM)
    return pl.pallas_call(
        functools.partial(kernel, chips, rows, parts),
        out_shape=jax.ShapeDtypeStruct((rows // 2, out_width), bf16),
        in_specs=[pl.BlockSpec(memory_space=pltpu.SMEM)] + [anywhere] * 4,
        out_specs=pl.BlockSpec(memory_space=pltpu.VMEM),
        scratch_shapes=[
            pltpu.VMEM((count, HEAD_DIM), bf16),
            pltpu.VMEM((chips, 2, 2, rows, HEAD_DIM), bf16),
            pltpu.VMEM((HEAD_DIM, count), f32),
            pltpu.VMEM((1, count), f32),
            pltpu.VMEM((1, count), f32),
            pltpu.VMEM((1, count), jnp.int32),
            pltpu.VMEM((count, HEAD_DIM), bf16),
            pltpu.VMEM((first, width), bf16),
            pltpu.VMEM((rows - first, width), bf16),
            pltpu.VMEM((width, out_width), bf16),
            pltpu.VMEM((first, out_width), f32),
            pltpu.VMEM((parts, first, out_width // parts), bf16),
            pltpu.VMEM((parts, first, out_width // parts), bf16),
            dma((4,)),
            dma,
            dma((2, chips)),
            dma((2, chips)),
            dma((chips, 2)),
            dma((chips, 2)),
            dma((chips,)),
            dma((chips,)),
            dma((2,)),
            dma((2, chips)),
            dma((2, chips)),
            dma((parts,)),
            dma((parts,)),
        ],
        compiler_params=pltpu.CompilerParams(
            collective_id=0, has_side_effects=True, vmem_limit_bytes=60 * 1024 * 1024
        ),
        cost_estimate=pl.CostEstimate(
            flops=8 * count * count * HEAD_DIM + 2 * rows * width * out_width,
            bytes_accessed=2 * (3 * rows * width + width * out_width),
            transcendentals=2 * count * count,
        ),
        name="exchange_attend_project",
    )(block_pos, queries, keys, values, w_out)


def solution(mesh):
    chips = mesh.shape["ctx"] // 2

    def body(queries, keys, values, block_pos, w_out):
        fits = mesh.shape["help"] == 2 and queries.shape[1] == chips * HEAD_DIM
        if fits and chips & (chips - 1) == 0 and queries.shape[0] % 16 == 0:
            return exchanged_body(chips, queries, keys, values, block_pos, w_out)
        return gathered_body(queries, keys, values, block_pos, w_out)

    in_specs = (P("ctx", "help"), P("ctx", "help"), P("ctx", "help"), P(), P("help", None))
    out_specs = P(("ctx", "help"), None)
    return jax.shard_map(body, mesh=mesh, in_specs=in_specs, out_specs=out_specs, check_vma=False)
```

```python
import functools
import math

import jax
import jax.numpy as jnp
from jax import lax
from jax.experimental import pallas as pl
from jax.experimental.pallas import tpu as pltpu
from jax.sharding import PartitionSpec as P

HEAD_DIM = 128
MESH = pl.DeviceIdType.MESH


def gathered_body(queries, keys, values, block_pos, w_out):
    n_ctx = lax.axis_size("ctx")
    device = lax.axis_index("ctx")
    rows, width = queries.shape
    heads = width // HEAD_DIM
    scale = 1.0 / HEAD_DIM**0.5
    own_block = jnp.sum(jnp.where(jnp.arange(n_ctx) == device, block_pos, 0))
    query_pos = own_block * rows + jnp.arange(rows, dtype=jnp.int32)
    whole_keys = lax.all_gather(keys, "ctx", axis=0, tiled=True)
    whole_values = lax.all_gather(values, "ctx", axis=0, tiled=True)
    count = whole_keys.shape[0]
    key_pos = (block_pos[:, None] * rows + jnp.arange(rows, dtype=jnp.int32)[None, :]).reshape(count)
    query_heads = queries.reshape(rows, heads, HEAD_DIM)
    key_heads = whole_keys.reshape(count, heads, HEAD_DIM)
    value_heads = whole_values.reshape(count, heads, HEAD_DIM)
    scores = (
        jnp.einsum("qhd,khd->hqk", query_heads, key_heads, preferred_element_type=jnp.float32)
        * scale
    )
    visible = key_pos[None, None, :] <= query_pos[None, :, None]
    top = jnp.max(jnp.where(visible, scores, -1e30), axis=2)
    weights = jnp.where(visible, jnp.exp(scores - top[:, :, None]), 0.0)
    total = jnp.sum(weights, axis=2)
    summed = jnp.einsum(
        "hqk,khd->hqd",
        weights.astype(jnp.bfloat16),
        value_heads,
        preferred_element_type=jnp.float32,
    )
    result = summed / total[:, :, None]
    attended = jnp.transpose(result, (1, 0, 2)).reshape(rows, width).astype(jnp.bfloat16)
    return lax.psum_scatter(
        jnp.dot(attended, w_out, preferred_element_type=jnp.float32).astype(jnp.bfloat16),
        "help",
        scatter_dimension=0,
        tiled=True,
    )


def column_spans(base, width):
    spans = []
    while width:
        lanes = width if width <= 384 else 256
        spans.append((base, lanes))
        base, width = base + lanes, width - lanes
    return tuple(spans)


def kernel(
    chips, rows, parts,
    bp_ref, q_hbm, k_hbm, v_hbm, w_hbm, out_ref,
    qbuf, kv, acc, top, total, qpos, osend, att_a, att_b, att_c, wbuf, part,
    psend_a, psend_b, precv_a, precv_b,
    own_sem, w_sem, q_send, q_recv, kv_send, kv_recv, relay_send, relay_recv,
    o_own, o_send, o_recv, p_send, p_recv,
):
    ctx = lax.axis_index("ctx")
    helper = lax.axis_index("help")
    chip = lax.div(ctx, 2)
    core = lax.rem(ctx, 2)
    sibling = chip * 2 + (1 - core)
    half = rows // 2
    att = (att_a, att_b, att_c)
    sets = range(3)
    size = tuple(ref.shape[0] for ref in att)
    swapped = size[0] + size[1]
    start = ((1 - helper) * size[2], (1 - helper) * size[2] + size[0], helper * swapped)
    base = (0, chips * size[0], chips * swapped)
    spans = tuple(column_spans(base[i], chips * size[i]) for i in sets)
    psend, precv = (psend_a, psend_b), (precv_a, precv_b)
    fold = math.log2(math.e) / HEAD_DIM**0.5

    def peer(step):
        found = 0
        for bit in range(chips.bit_length() - 1):
            mine = lax.rem(lax.div(chip, 1 << bit), 2)
            other = step // (1 << bit) % 2 if isinstance(step, int) else lax.rem(
                lax.div(step, 1 << bit), 2
            )
            found = found + (mine + other - 2 * mine * other) * (1 << bit)
        return found

    def head_of(ref, which):
        return ref.at[:, pl.ds(pl.multiple_of(which * HEAD_DIM, HEAD_DIM), HEAD_DIM)]

    def query_rows(which, head):
        return q_hbm.at[
            pl.ds(pl.multiple_of(start[which], 16), size[which]),
            pl.ds(pl.multiple_of(head * HEAD_DIM, HEAD_DIM), HEAD_DIM),
        ]

    def held_rows(ref, which, block):
        return ref.at[pl.ds(pl.multiple_of(base[which] + block * size[which], 16), size[which]), :]

    w_copy = pltpu.make_async_copy(w_hbm, wbuf, w_sem)
    own = [
        pltpu.make_async_copy(head_of(k_hbm, chip), kv.at[chip, core, 0], own_sem.at[0]),
        pltpu.make_async_copy(head_of(v_hbm, chip), kv.at[chip, core, 1], own_sem.at[1]),
    ] + [
        pltpu.make_async_copy(query_rows(i, chip), held_rows(qbuf, i, chip), own_sem.at[2 + i])
        for i in sets
    ]
    for copy in own:
        copy.start()
    w_copy.start()

    barrier = pltpu.get_barrier_semaphore()
    for step in range(1, chips):
        pl.semaphore_signal(
            barrier, inc=1, device_id=(peer(step) * 2 + core, helper), device_id_type=MESH
        )
    pl.semaphore_signal(barrier, inc=1, device_id=(sibling, helper), device_id_type=MESH)
    pl.semaphore_signal(barrier, inc=1, device_id=(ctx, 1 - helper), device_id_type=MESH)
    pl.semaphore_wait(barrier, chips + 1)

    def q_copy(which, step, source):
        return pltpu.make_async_remote_copy(
            src_ref=query_rows(which, peer(step)),
            dst_ref=held_rows(qbuf, which, source),
            send_sem=q_send.at[which, step],
            recv_sem=q_recv.at[which, source],
            device_id=(peer(step) * 2 + core, helper),
            device_id_type=MESH,
        )

    def kv_copy(step, source, which):
        return pltpu.make_async_remote_copy(
            src_ref=head_of((k_hbm, v_hbm)[which], peer(step)),
            dst_ref=kv.at[source, core, which],
            send_sem=kv_send.at[step, which],
            recv_sem=kv_recv.at[source, which],
            device_id=(peer(step) * 2 + core, helper),
            device_id_type=MESH,
        )

    def relay(source, from_core):
        return pltpu.make_async_remote_copy(
            src_ref=kv.at[source, from_core],
            dst_ref=kv.at[source, from_core],
            send_sem=relay_send.at[source],
            recv_sem=relay_recv.at[source],
            device_id=(sibling, helper),
            device_id_type=MESH,
        )

    for step in range(1, chips):
        for which in (0, 1):
            q_copy(which, step, chip).start()
    for step in range(1, chips):
        kv_copy(step, chip, 0).start()
        kv_copy(step, chip, 1).start()
    for step in range(1, chips):
        q_copy(2, step, chip).start()

    lane = lax.broadcasted_iota(jnp.int32, qpos.shape, 1)
    position = jnp.zeros(qpos.shape, jnp.int32)
    for which in sets:
        for block in range(chips):
            begin = base[which] + block * size[which]
            inside = (lane >= begin) & (lane < begin + size[which])
            place = bp_ref[block * 2 + core] * rows + start[which] - begin
            position = jnp.where(inside, lane + place, position)
    qpos[...] = position
    acc[...] = jnp.zeros_like(acc)
    total[...] = jnp.zeros_like(total)
    top[...] = jnp.full(top.shape, -1e9, jnp.float32)

    def attend(source, chosen):
        keys = kv[source, :, 0].reshape(2 * rows, HEAD_DIM)
        values = kv[source, :, 1].reshape(2 * rows, HEAD_DIM).T
        first = bp_ref[source * 2] * rows
        second = bp_ref[source * 2 + 1] * rows
        for begin, lanes in sum((spans[i] for i in chosen), ()):
            cols = pl.ds(begin, lanes)
            raw = lax.dot_general(
                keys, qbuf[cols, :], (((1,), (1,)), ((), ())), preferred_element_type=jnp.float32
            )
            inner = lax.broadcasted_iota(jnp.int32, (rows, lanes), 0)
            place = qpos[:, cols]
            raw = jnp.concatenate(
                [
                    jnp.where(inner <= place - first, raw[:rows], -1e30),
                    jnp.where(inner <= place - second, raw[rows:], -1e30),
                ],
                axis=0,
            )
            before = top[:, cols]
            after = jnp.maximum(before, jnp.max(raw, axis=0, keepdims=True))
            weights = jnp.exp2(raw * fold - after * fold)
            keep = jnp.exp2((before - after) * fold)
            top[:, cols] = after
            total[:, cols] = total[:, cols] * keep + jnp.sum(weights, axis=0, keepdims=True)
            acc[:, cols] = acc[:, cols] * keep + jnp.dot(
                values, weights.astype(jnp.bfloat16), preferred_element_type=jnp.float32
            )

    own[0].wait()
    own[1].wait()
    relay(chip, core).start()
    def take_queries(which):
        own[2 + which].wait()
        for step in range(1, chips):
            q_copy(which, step, peer(step)).wait_recv()

    take_queries(0)
    take_queries(1)

    def turn(index):
        return index

    def one_step(index, carry):
        step = turn(index)
        source = peer(step)
        kv_copy(step, source, 0).wait_recv()
        kv_copy(step, source, 1).wait_recv()
        relay(source, core).start()
        done = lax.select(index == 1, chip, peer(turn(index - 1)))
        relay(done, 1 - core).wait_recv()
        attend(done, (0, 1))
        return carry

    lax.fori_loop(1, chips, one_step, 0)
    last = peer(turn(chips - 1))
    relay(last, 1 - core).wait_recv()

    def o_copy(which, step, head):
        return pltpu.make_async_remote_copy(
            src_ref=held_rows(osend, which, peer(step)),
            dst_ref=head_of(att[which], head),
            send_sem=o_send.at[which, step],
            recv_sem=o_recv.at[which, head],
            device_id=(peer(step) * 2 + core, helper),
            device_id_type=MESH,
        )

    def o_local(which):
        return pltpu.make_async_copy(
            held_rows(osend, which, chip), head_of(att[which], chip), o_own.at[which]
        )

    def give(which):
        for begin, lanes in spans[which]:
            cols = pl.ds(begin, lanes)
            result = acc[:, cols] * (1.0 / total[:, cols])
            osend[cols, :] = result.T.astype(jnp.bfloat16)
        for step in range(1, chips):
            o_copy(which, step, chip).start()
        o_local(which).start()

    def take(which):
        o_local(which).wait()
        for step in range(1, chips):
            o_copy(which, step, peer(step)).wait_recv()

    for which in range(2):
        attend(last, (which,))
        give(which)

    def second_pass(source, carry):
        attend(source, (2,))
        return carry

    wide = w_hbm.shape[1] // parts

    def p_copy(which, index):
        return pltpu.make_async_remote_copy(
            src_ref=psend[which].at[index],
            dst_ref=precv[which].at[index],
            send_sem=p_send.at[which, index],
            recv_sem=p_recv.at[which, index],
            device_id=(ctx, 1 - helper),
            device_id_type=MESH,
        )

    def project_early(which):
        take(which)
        held = pl.ds(which * size[0], size[which])
        for index in range(parts):
            cols = pl.ds(index * wide, wide)
            product = jnp.dot(att[which][...], wbuf[:, cols], preferred_element_type=jnp.float32)
            part[held, cols] = product
            psend[which][index] = product.astype(jnp.bfloat16)
            p_copy(which, index).start()

    w_copy.wait()
    take_queries(2)
    cut = chips // 2
    lax.fori_loop(0, cut, second_pass, 0)
    if cut < chips:
        project_early(0)
        lax.fori_loop(cut, chips, second_pass, 0)
    give(2)
    if cut == chips:
        project_early(0)
    project_early(1)
    take(2)
    spare = swapped - half
    for index in range(parts):
        cols = pl.ds(index * wide, wide)
        product = jnp.dot(att_c[...], wbuf[:, cols], preferred_element_type=jnp.float32)
        part[:half, cols] = jnp.where(
            helper == 0,
            jnp.concatenate([product, part[:spare, cols]], axis=0),
            jnp.concatenate([part[half:, cols], product], axis=0),
        )
    for index in range(parts):
        cols = pl.ds(index * wide, wide)
        for which in range(2):
            p_copy(which, index).wait_recv()
        theirs = jnp.concatenate(
            [precv[i][index].astype(jnp.float32) for i in range(2)], axis=0
        )
        theirs = jnp.where(helper == 0, theirs[:half], theirs[spare:])
        out_ref[:, cols] = (part[:half, cols] + theirs).astype(jnp.bfloat16)

    for step in range(1, chips):
        for which in sets:
            q_copy(which, step, chip).wait_send()
            o_copy(which, step, chip).wait_send()
        for which in range(2):
            kv_copy(step, chip, which).wait_send()
    for source in range(chips):
        relay(source, core).wait_send()
    for which in range(2):
        for index in range(parts):
            p_copy(which, index).wait_send()


def exchanged_body(chips, queries, keys, values, block_pos, w_out):
    rows, width = queries.shape
    out_width = w_out.shape[1]
    count = chips * rows
    parts = 2
    first = -(-(rows // 2) // 16) * 16
    early = 48
    bf16, f32 = jnp.bfloat16, jnp.float32
    dma = pltpu.SemaphoreType.DMA
    anywhere = pl.BlockSpec(memory_space=pltpu.HBM)
    return pl.pallas_call(
        functools.partial(kernel, chips, rows, parts),
        out_shape=jax.ShapeDtypeStruct((rows // 2, out_width), bf16),
        in_specs=[pl.BlockSpec(memory_space=pltpu.SMEM)] + [anywhere] * 4,
        out_specs=pl.BlockSpec(memory_space=pltpu.VMEM),
        scratch_shapes=[
            pltpu.VMEM((count, HEAD_DIM), bf16),
            pltpu.VMEM((chips, 2, 2, rows, HEAD_DIM), bf16),
            pltpu.VMEM((HEAD_DIM, count), f32),
            pltpu.VMEM((1, count), f32),
            pltpu.VMEM((1, count), f32),
            pltpu.VMEM((1, count), jnp.int32),
            pltpu.VMEM((count, HEAD_DIM), bf16),
            pltpu.VMEM((early, width), bf16),
            pltpu.VMEM((first - early, width), bf16),
            pltpu.VMEM((rows - first, width), bf16),
            pltpu.VMEM((width, out_width), bf16),
            pltpu.VMEM((first, out_width), f32),
            pltpu.VMEM((parts, early, out_width // parts), bf16),
            pltpu.VMEM((parts, first - early, out_width // parts), bf16),
            pltpu.VMEM((parts, early, out_width // parts), bf16),
            pltpu.VMEM((parts, first - early, out_width // parts), bf16),
            dma((5,)),
            dma,
            dma((3, chips)),
            dma((3, chips)),
            dma((chips, 2)),
            dma((chips, 2)),
            dma((chips,)),
            dma((chips,)),
            dma((3,)),
            dma((3, chips)),
            dma((3, chips)),
            dma((2, parts)),
            dma((2, parts)),
        ],
        compiler_params=pltpu.CompilerParams(
            collective_id=0, has_side_effects=True, vmem_limit_bytes=60 * 1024 * 1024
        ),
        cost_estimate=pl.CostEstimate(
            flops=8 * count * count * HEAD_DIM + 2 * rows * width * out_width,
            bytes_accessed=2 * (3 * rows * width + width * out_width),
            transcendentals=2 * count * count,
        ),
        name="exchange_attend_project",
    )(block_pos, queries, keys, values, w_out)


def solution(mesh):
    chips = mesh.shape["ctx"] // 2

    def body(queries, keys, values, block_pos, w_out):
        fits = mesh.shape["help"] == 2 and queries.shape[1] == chips * HEAD_DIM
        if fits and chips & (chips - 1) == 0 and queries.shape[0] % 16 == 0:
            return exchanged_body(chips, queries, keys, values, block_pos, w_out)
        return gathered_body(queries, keys, values, block_pos, w_out)

    in_specs = (P("ctx", "help"), P("ctx", "help"), P("ctx", "help"), P(), P("help", None))
    out_specs = P(("ctx", "help"), None)
    return jax.shard_map(body, mesh=mesh, in_specs=in_specs, out_specs=out_specs, check_vma=False)
```

```python
import functools
import math

import jax
import jax.numpy as jnp
from jax import lax
from jax.experimental import pallas as pl
from jax.experimental.pallas import tpu as pltpu
from jax.sharding import PartitionSpec as P

HEAD_DIM = 128
MESH = pl.DeviceIdType.MESH


def gathered_body(queries, keys, values, block_pos, w_out):
    n_ctx = lax.axis_size("ctx")
    device = lax.axis_index("ctx")
    rows, width = queries.shape
    heads = width // HEAD_DIM
    scale = 1.0 / HEAD_DIM**0.5
    own_block = jnp.sum(jnp.where(jnp.arange(n_ctx) == device, block_pos, 0))
    query_pos = own_block * rows + jnp.arange(rows, dtype=jnp.int32)
    whole_keys = lax.all_gather(keys, "ctx", axis=0, tiled=True)
    whole_values = lax.all_gather(values, "ctx", axis=0, tiled=True)
    count = whole_keys.shape[0]
    key_pos = (block_pos[:, None] * rows + jnp.arange(rows, dtype=jnp.int32)[None, :]).reshape(count)
    query_heads = queries.reshape(rows, heads, HEAD_DIM)
    key_heads = whole_keys.reshape(count, heads, HEAD_DIM)
    value_heads = whole_values.reshape(count, heads, HEAD_DIM)
    scores = (
        jnp.einsum("qhd,khd->hqk", query_heads, key_heads, preferred_element_type=jnp.float32)
        * scale
    )
    visible = key_pos[None, None, :] <= query_pos[None, :, None]
    top = jnp.max(jnp.where(visible, scores, -1e30), axis=2)
    weights = jnp.where(visible, jnp.exp(scores - top[:, :, None]), 0.0)
    total = jnp.sum(weights, axis=2)
    summed = jnp.einsum(
        "hqk,khd->hqd",
        weights.astype(jnp.bfloat16),
        value_heads,
        preferred_element_type=jnp.float32,
    )
    result = summed / total[:, :, None]
    attended = jnp.transpose(result, (1, 0, 2)).reshape(rows, width).astype(jnp.bfloat16)
    return lax.psum_scatter(
        jnp.dot(attended, w_out, preferred_element_type=jnp.float32).astype(jnp.bfloat16),
        "help",
        scatter_dimension=0,
        tiled=True,
    )


def column_spans(base, width):
    spans = []
    while width:
        lanes = width if width <= 384 else 256
        spans.append((base, lanes))
        base, width = base + lanes, width - lanes
    return tuple(spans)


def kernel(
    chips, rows, parts,
    bp_ref, q_hbm, k_hbm, v_hbm, w_hbm, out_ref,
    qbuf, kv, acc, top, total, qpos, osend, att_a, att_b, att_c, wbuf, part,
    psend_a, psend_b, precv_a, precv_b,
    own_sem, w_sem, q_send, q_recv, kv_send, kv_recv, relay_send, relay_recv,
    o_own, o_send, o_recv, p_send, p_recv,
):
    ctx = lax.axis_index("ctx")
    helper = lax.axis_index("help")
    chip = lax.div(ctx, 2)
    core = lax.rem(ctx, 2)
    sibling = chip * 2 + (1 - core)
    half = rows // 2
    att = (att_a, att_b, att_c)
    sets = range(3)
    size = tuple(ref.shape[0] for ref in att)
    swapped = size[0] + size[1]
    start = ((1 - helper) * size[2], (1 - helper) * size[2] + size[0], helper * swapped)
    base = (0, chips * size[0], chips * swapped)
    spans = tuple(column_spans(base[i], chips * size[i]) for i in sets)
    psend, precv = (psend_a, psend_b), (precv_a, precv_b)
    fold = math.log2(math.e) / HEAD_DIM**0.5

    def peer(step):
        found = 0
        for bit in range(chips.bit_length() - 1):
            mine = lax.rem(lax.div(chip, 1 << bit), 2)
            other = step // (1 << bit) % 2 if isinstance(step, int) else lax.rem(
                lax.div(step, 1 << bit), 2
            )
            found = found + (mine + other - 2 * mine * other) * (1 << bit)
        return found

    def head_of(ref, which):
        return ref.at[:, pl.ds(pl.multiple_of(which * HEAD_DIM, HEAD_DIM), HEAD_DIM)]

    def query_rows(which, head):
        return q_hbm.at[
            pl.ds(pl.multiple_of(start[which], 16), size[which]),
            pl.ds(pl.multiple_of(head * HEAD_DIM, HEAD_DIM), HEAD_DIM),
        ]

    def held_rows(ref, which, block):
        return ref.at[pl.ds(pl.multiple_of(base[which] + block * size[which], 16), size[which]), :]

    w_copy = pltpu.make_async_copy(w_hbm, wbuf, w_sem)
    own = [
        pltpu.make_async_copy(head_of(k_hbm, chip), kv.at[chip, core, 0], own_sem.at[0]),
        pltpu.make_async_copy(head_of(v_hbm, chip), kv.at[chip, core, 1], own_sem.at[1]),
    ] + [
        pltpu.make_async_copy(query_rows(i, chip), held_rows(qbuf, i, chip), own_sem.at[2 + i])
        for i in sets
    ]
    for copy in own:
        copy.start()
    w_copy.start()

    barrier = pltpu.get_barrier_semaphore()
    for step in range(1, chips):
        pl.semaphore_signal(
            barrier, inc=1, device_id=(peer(step) * 2 + core, helper), device_id_type=MESH
        )
    pl.semaphore_signal(barrier, inc=1, device_id=(sibling, helper), device_id_type=MESH)
    pl.semaphore_signal(barrier, inc=1, device_id=(ctx, 1 - helper), device_id_type=MESH)
    pl.semaphore_wait(barrier, chips + 1)

    def q_copy(which, step, source):
        return pltpu.make_async_remote_copy(
            src_ref=query_rows(which, peer(step)),
            dst_ref=held_rows(qbuf, which, source),
            send_sem=q_send.at[which, step],
            recv_sem=q_recv.at[which, source],
            device_id=(peer(step) * 2 + core, helper),
            device_id_type=MESH,
        )

    def kv_copy(step, source, which):
        return pltpu.make_async_remote_copy(
            src_ref=head_of((k_hbm, v_hbm)[which], peer(step)),
            dst_ref=kv.at[source, core, which],
            send_sem=kv_send.at[step, which],
            recv_sem=kv_recv.at[source, which],
            device_id=(peer(step) * 2 + core, helper),
            device_id_type=MESH,
        )

    def relay(source, from_core):
        return pltpu.make_async_remote_copy(
            src_ref=kv.at[source, from_core],
            dst_ref=kv.at[source, from_core],
            send_sem=relay_send.at[source],
            recv_sem=relay_recv.at[source],
            device_id=(sibling, helper),
            device_id_type=MESH,
        )

    for step in range(1, chips):
        for which in (0, 1):
            q_copy(which, step, chip).start()
    for step in range(1, chips):
        kv_copy(step, chip, 0).start()
        kv_copy(step, chip, 1).start()

    lane = lax.broadcasted_iota(jnp.int32, qpos.shape, 1)
    position = jnp.zeros(qpos.shape, jnp.int32)
    for which in sets:
        for block in range(chips):
            begin = base[which] + block * size[which]
            inside = (lane >= begin) & (lane < begin + size[which])
            place = bp_ref[block * 2 + core] * rows + start[which] - begin
            position = jnp.where(inside, lane + place, position)
    qpos[...] = position
    acc[...] = jnp.zeros_like(acc)
    total[...] = jnp.zeros_like(total)
    top[...] = jnp.full(top.shape, -1e9, jnp.float32)

    def attend(source, chosen):
        keys = kv[source, :, 0].reshape(2 * rows, HEAD_DIM)
        values = kv[source, :, 1].reshape(2 * rows, HEAD_DIM).T
        first = bp_ref[source * 2] * rows
        second = bp_ref[source * 2 + 1] * rows
        for begin, lanes in sum((spans[i] for i in chosen), ()):
            cols = pl.ds(begin, lanes)
            raw = lax.dot_general(
                keys, qbuf[cols, :], (((1,), (1,)), ((), ())), preferred_element_type=jnp.float32
            )
            inner = lax.broadcasted_iota(jnp.int32, (rows, lanes), 0)
            place = qpos[:, cols]
            raw = jnp.concatenate(
                [
                    jnp.where(inner <= place - first, raw[:rows], -1e30),
                    jnp.where(inner <= place - second, raw[rows:], -1e30),
                ],
                axis=0,
            )
            before = top[:, cols]
            after = jnp.maximum(before, jnp.max(raw, axis=0, keepdims=True))
            weights = jnp.exp2(raw * fold - after * fold)
            keep = jnp.exp2((before - after) * fold)
            top[:, cols] = after
            total[:, cols] = total[:, cols] * keep + jnp.sum(weights, axis=0, keepdims=True)
            acc[:, cols] = acc[:, cols] * keep + jnp.dot(
                values, weights.astype(jnp.bfloat16), preferred_element_type=jnp.float32
            )

    own[0].wait()
    own[1].wait()
    relay(chip, core).start()
    def take_queries(which):
        own[2 + which].wait()
        for step in range(1, chips):
            q_copy(which, step, peer(step)).wait_recv()

    take_queries(0)
    take_queries(1)

    def turn(index):
        return index

    def one_step(index, carry):
        step = turn(index)
        source = peer(step)
        kv_copy(step, source, 0).wait_recv()
        kv_copy(step, source, 1).wait_recv()
        relay(source, core).start()
        done = lax.select(index == 1, chip, peer(turn(index - 1)))
        relay(done, 1 - core).wait_recv()
        attend(done, (0, 1))
        return carry

    lax.fori_loop(1, chips - 2, one_step, 0)
    for step in range(1, chips):
        q_copy(2, step, chip).start()
    lax.fori_loop(chips - 2, chips, one_step, 0)
    last = peer(turn(chips - 1))
    relay(last, 1 - core).wait_recv()

    def o_copy(which, step, head):
        return pltpu.make_async_remote_copy(
            src_ref=held_rows(osend, which, peer(step)),
            dst_ref=head_of(att[which], head),
            send_sem=o_send.at[which, step],
            recv_sem=o_recv.at[which, head],
            device_id=(peer(step) * 2 + core, helper),
            device_id_type=MESH,
        )

    def o_local(which):
        return pltpu.make_async_copy(
            held_rows(osend, which, chip), head_of(att[which], chip), o_own.at[which]
        )

    def give(which):
        for begin, lanes in spans[which]:
            cols = pl.ds(begin, lanes)
            result = acc[:, cols] * (1.0 / total[:, cols])
            osend[cols, :] = result.T.astype(jnp.bfloat16)
        for step in range(1, chips):
            o_copy(which, step, chip).start()
        o_local(which).start()

    def take(which):
        o_local(which).wait()
        for step in range(1, chips):
            o_copy(which, step, peer(step)).wait_recv()

    for which in range(2):
        attend(last, (which,))
        give(which)

    def second_pass(source, carry):
        attend(source, (2,))
        return carry

    wide = w_hbm.shape[1] // parts

    def p_copy(which, index):
        return pltpu.make_async_remote_copy(
            src_ref=psend[which].at[index],
            dst_ref=precv[which].at[index],
            send_sem=p_send.at[which, index],
            recv_sem=p_recv.at[which, index],
            device_id=(ctx, 1 - helper),
            device_id_type=MESH,
        )

    def project_early(which):
        take(which)
        held = pl.ds(which * size[0], size[which])
        for index in range(parts):
            cols = pl.ds(index * wide, wide)
            product = jnp.dot(att[which][...], wbuf[:, cols], preferred_element_type=jnp.float32)
            part[held, cols] = product
            psend[which][index] = product.astype(jnp.bfloat16)
            p_copy(which, index).start()

    w_copy.wait()
    take_queries(2)
    cut = chips // 2
    lax.fori_loop(0, cut, second_pass, 0)
    if cut < chips:
        project_early(0)
        lax.fori_loop(cut, chips, second_pass, 0)
    give(2)
    if cut == chips:
        project_early(0)
    project_early(1)
    take(2)
    spare = swapped - half
    for index in range(parts):
        cols = pl.ds(index * wide, wide)
        product = jnp.dot(att_c[...], wbuf[:, cols], preferred_element_type=jnp.float32)
        part[:half, cols] = jnp.where(
            helper == 0,
            jnp.concatenate([product, part[:spare, cols]], axis=0),
            jnp.concatenate([part[half:, cols], product], axis=0),
        )
    for index in range(parts):
        cols = pl.ds(index * wide, wide)
        for which in range(2):
            p_copy(which, index).wait_recv()
        theirs = jnp.concatenate(
            [precv[i][index].astype(jnp.float32) for i in range(2)], axis=0
        )
        theirs = jnp.where(helper == 0, theirs[:half], theirs[spare:])
        out_ref[:, cols] = (part[:half, cols] + theirs).astype(jnp.bfloat16)

    for step in range(1, chips):
        for which in sets:
            q_copy(which, step, chip).wait_send()
            o_copy(which, step, chip).wait_send()
        for which in range(2):
            kv_copy(step, chip, which).wait_send()
    for source in range(chips):
        relay(source, core).wait_send()
    for which in range(2):
        for index in range(parts):
            p_copy(which, index).wait_send()


def exchanged_body(chips, queries, keys, values, block_pos, w_out):
    rows, width = queries.shape
    out_width = w_out.shape[1]
    count = chips * rows
    parts = 2
    first = -(-(rows // 2) // 16) * 16
    early = 48
    bf16, f32 = jnp.bfloat16, jnp.float32
    dma = pltpu.SemaphoreType.DMA
    anywhere = pl.BlockSpec(memory_space=pltpu.HBM)
    return pl.pallas_call(
        functools.partial(kernel, chips, rows, parts),
        out_shape=jax.ShapeDtypeStruct((rows // 2, out_width), bf16),
        in_specs=[pl.BlockSpec(memory_space=pltpu.SMEM)] + [anywhere] * 4,
        out_specs=pl.BlockSpec(memory_space=pltpu.VMEM),
        scratch_shapes=[
            pltpu.VMEM((count, HEAD_DIM), bf16),
            pltpu.VMEM((chips, 2, 2, rows, HEAD_DIM), bf16),
            pltpu.VMEM((HEAD_DIM, count), f32),
            pltpu.VMEM((1, count), f32),
            pltpu.VMEM((1, count), f32),
            pltpu.VMEM((1, count), jnp.int32),
            pltpu.VMEM((count, HEAD_DIM), bf16),
            pltpu.VMEM((early, width), bf16),
            pltpu.VMEM((first - early, width), bf16),
            pltpu.VMEM((rows - first, width), bf16),
            pltpu.VMEM((width, out_width), bf16),
            pltpu.VMEM((first, out_width), f32),
            pltpu.VMEM((parts, early, out_width // parts), bf16),
            pltpu.VMEM((parts, first - early, out_width // parts), bf16),
            pltpu.VMEM((parts, early, out_width // parts), bf16),
            pltpu.VMEM((parts, first - early, out_width // parts), bf16),
            dma((5,)),
            dma,
            dma((3, chips)),
            dma((3, chips)),
            dma((chips, 2)),
            dma((chips, 2)),
            dma((chips,)),
            dma((chips,)),
            dma((3,)),
            dma((3, chips)),
            dma((3, chips)),
            dma((2, parts)),
            dma((2, parts)),
        ],
        compiler_params=pltpu.CompilerParams(
            collective_id=0, has_side_effects=True, vmem_limit_bytes=60 * 1024 * 1024
        ),
        cost_estimate=pl.CostEstimate(
            flops=8 * count * count * HEAD_DIM + 2 * rows * width * out_width,
            bytes_accessed=2 * (3 * rows * width + width * out_width),
            transcendentals=2 * count * count,
        ),
        name="exchange_attend_project",
    )(block_pos, queries, keys, values, w_out)


def solution(mesh):
    chips = mesh.shape["ctx"] // 2

    def body(queries, keys, values, block_pos, w_out):
        fits = mesh.shape["help"] == 2 and queries.shape[1] == chips * HEAD_DIM
        if fits and chips & (chips - 1) == 0 and queries.shape[0] % 16 == 0:
            return exchanged_body(chips, queries, keys, values, block_pos, w_out)
        return gathered_body(queries, keys, values, block_pos, w_out)

    in_specs = (P("ctx", "help"), P("ctx", "help"), P("ctx", "help"), P(), P("help", None))
    out_specs = P(("ctx", "help"), None)
    return jax.shard_map(body, mesh=mesh, in_specs=in_specs, out_specs=out_specs, check_vma=False)
```

```python
import functools
import math

import jax
import jax.numpy as jnp
from jax import lax
from jax.experimental import pallas as pl
from jax.experimental.pallas import tpu as pltpu
from jax.sharding import PartitionSpec as P

HEAD_DIM = 128
MESH = pl.DeviceIdType.MESH


def gathered_body(queries, keys, values, block_pos, w_out):
    n_ctx = lax.axis_size("ctx")
    device = lax.axis_index("ctx")
    rows, width = queries.shape
    heads = width // HEAD_DIM
    scale = 1.0 / HEAD_DIM**0.5
    own_block = jnp.sum(jnp.where(jnp.arange(n_ctx) == device, block_pos, 0))
    query_pos = own_block * rows + jnp.arange(rows, dtype=jnp.int32)
    whole_keys = lax.all_gather(keys, "ctx", axis=0, tiled=True)
    whole_values = lax.all_gather(values, "ctx", axis=0, tiled=True)
    count = whole_keys.shape[0]
    key_pos = (block_pos[:, None] * rows + jnp.arange(rows, dtype=jnp.int32)[None, :]).reshape(count)
    query_heads = queries.reshape(rows, heads, HEAD_DIM)
    key_heads = whole_keys.reshape(count, heads, HEAD_DIM)
    value_heads = whole_values.reshape(count, heads, HEAD_DIM)
    scores = (
        jnp.einsum("qhd,khd->hqk", query_heads, key_heads, preferred_element_type=jnp.float32)
        * scale
    )
    visible = key_pos[None, None, :] <= query_pos[None, :, None]
    top = jnp.max(jnp.where(visible, scores, -1e30), axis=2)
    weights = jnp.where(visible, jnp.exp(scores - top[:, :, None]), 0.0)
    total = jnp.sum(weights, axis=2)
    summed = jnp.einsum(
        "hqk,khd->hqd",
        weights.astype(jnp.bfloat16),
        value_heads,
        preferred_element_type=jnp.float32,
    )
    result = summed / total[:, :, None]
    attended = jnp.transpose(result, (1, 0, 2)).reshape(rows, width).astype(jnp.bfloat16)
    return lax.psum_scatter(
        jnp.dot(attended, w_out, preferred_element_type=jnp.float32).astype(jnp.bfloat16),
        "help",
        scatter_dimension=0,
        tiled=True,
    )


def column_spans(base, width):
    spans = []
    while width:
        lanes = width if width <= 384 else 256
        spans.append((base, lanes))
        base, width = base + lanes, width - lanes
    return tuple(spans)


def kernel(
    chips, rows, parts,
    bp_ref, q_hbm, k_hbm, v_hbm, w_hbm, out_ref,
    qbuf, kv, acc, top, total, qpos, osend, att_a, att_b, att_c, wbuf, part,
    psend_a, psend_b, precv_a, precv_b,
    own_sem, w_sem, q_send, q_recv, kv_send, kv_recv, relay_send, relay_recv,
    o_own, o_send, o_recv, p_send, p_recv,
):
    ctx = lax.axis_index("ctx")
    helper = lax.axis_index("help")
    chip = lax.div(ctx, 2)
    core = lax.rem(ctx, 2)
    sibling = chip * 2 + (1 - core)
    half = rows // 2
    att = (att_a, att_b, att_c)
    sets = range(3)
    size = tuple(ref.shape[0] for ref in att)
    swapped = size[0] + size[1]
    start = ((1 - helper) * size[2], (1 - helper) * size[2] + size[0], helper * swapped)
    base = (0, chips * size[0], chips * swapped)
    spans = tuple(column_spans(base[i], chips * size[i]) for i in sets)
    psend, precv = (psend_a, psend_b), (precv_a, precv_b)
    fold = math.log2(math.e) / HEAD_DIM**0.5

    def peer(step):
        found = 0
        for bit in range(chips.bit_length() - 1):
            mine = lax.rem(lax.div(chip, 1 << bit), 2)
            other = step // (1 << bit) % 2 if isinstance(step, int) else lax.rem(
                lax.div(step, 1 << bit), 2
            )
            found = found + (mine + other - 2 * mine * other) * (1 << bit)
        return found

    def head_of(ref, which):
        return ref.at[:, pl.ds(pl.multiple_of(which * HEAD_DIM, HEAD_DIM), HEAD_DIM)]

    def query_rows(which, head):
        return q_hbm.at[
            pl.ds(pl.multiple_of(start[which], 16), size[which]),
            pl.ds(pl.multiple_of(head * HEAD_DIM, HEAD_DIM), HEAD_DIM),
        ]

    def held_rows(ref, which, block):
        return ref.at[pl.ds(pl.multiple_of(base[which] + block * size[which], 16), size[which]), :]

    w_copy = pltpu.make_async_copy(w_hbm, wbuf, w_sem)
    own = [
        pltpu.make_async_copy(head_of(k_hbm, chip), kv.at[chip, core, 0], own_sem.at[0]),
        pltpu.make_async_copy(head_of(v_hbm, chip), kv.at[chip, core, 1], own_sem.at[1]),
    ] + [
        pltpu.make_async_copy(query_rows(i, chip), held_rows(qbuf, i, chip), own_sem.at[2 + i])
        for i in sets
    ]
    for copy in own:
        copy.start()
    w_copy.start()

    barrier = pltpu.get_barrier_semaphore()
    for step in range(1, chips):
        pl.semaphore_signal(
            barrier, inc=1, device_id=(peer(step) * 2 + core, helper), device_id_type=MESH
        )
    pl.semaphore_signal(barrier, inc=1, device_id=(sibling, helper), device_id_type=MESH)
    pl.semaphore_signal(barrier, inc=1, device_id=(ctx, 1 - helper), device_id_type=MESH)
    pl.semaphore_wait(barrier, chips + 1)

    def q_copy(which, step, source):
        return pltpu.make_async_remote_copy(
            src_ref=query_rows(which, peer(step)),
            dst_ref=held_rows(qbuf, which, source),
            send_sem=q_send.at[which, step],
            recv_sem=q_recv.at[which, source],
            device_id=(peer(step) * 2 + core, helper),
            device_id_type=MESH,
        )

    def kv_copy(step, source, which):
        return pltpu.make_async_remote_copy(
            src_ref=head_of((k_hbm, v_hbm)[which], peer(step)),
            dst_ref=kv.at[source, core, which],
            send_sem=kv_send.at[step, which],
            recv_sem=kv_recv.at[source, which],
            device_id=(peer(step) * 2 + core, helper),
            device_id_type=MESH,
        )

    def relay(source, from_core):
        return pltpu.make_async_remote_copy(
            src_ref=kv.at[source, from_core],
            dst_ref=kv.at[source, from_core],
            send_sem=relay_send.at[source],
            recv_sem=relay_recv.at[source],
            device_id=(sibling, helper),
            device_id_type=MESH,
        )

    for step in range(1, chips):
        for which in (0, 1):
            q_copy(which, step, chip).start()
    for step in [*range(chips // 2, chips), *range(1, chips // 2)]:
        kv_copy(step, chip, 0).start()
        kv_copy(step, chip, 1).start()

    lane = lax.broadcasted_iota(jnp.int32, qpos.shape, 1)
    position = jnp.zeros(qpos.shape, jnp.int32)
    for which in sets:
        for block in range(chips):
            begin = base[which] + block * size[which]
            inside = (lane >= begin) & (lane < begin + size[which])
            place = bp_ref[block * 2 + core] * rows + start[which] - begin
            position = jnp.where(inside, lane + place, position)
    qpos[...] = position
    acc[...] = jnp.zeros_like(acc)
    total[...] = jnp.zeros_like(total)
    top[...] = jnp.full(top.shape, -1e9, jnp.float32)

    def attend(source, chosen):
        keys = kv[source, :, 0].reshape(2 * rows, HEAD_DIM)
        values = kv[source, :, 1].reshape(2 * rows, HEAD_DIM).T
        first = bp_ref[source * 2] * rows
        second = bp_ref[source * 2 + 1] * rows
        for begin, lanes in sum((spans[i] for i in chosen), ()):
            cols = pl.ds(begin, lanes)
            raw = lax.dot_general(
                keys, qbuf[cols, :], (((1,), (1,)), ((), ())), preferred_element_type=jnp.float32
            )
            inner = lax.broadcasted_iota(jnp.int32, (rows, lanes), 0)
            place = qpos[:, cols]
            raw = jnp.concatenate(
                [
                    jnp.where(inner <= place - first, raw[:rows], -1e30),
                    jnp.where(inner <= place - second, raw[rows:], -1e30),
                ],
                axis=0,
            )
            before = top[:, cols]
            after = jnp.maximum(before, jnp.max(raw, axis=0, keepdims=True))
            weights = jnp.exp2(raw * fold - after * fold)
            keep = jnp.exp2((before - after) * fold)
            top[:, cols] = after
            total[:, cols] = total[:, cols] * keep + jnp.sum(weights, axis=0, keepdims=True)
            acc[:, cols] = acc[:, cols] * keep + jnp.dot(
                values, weights.astype(jnp.bfloat16), preferred_element_type=jnp.float32
            )

    own[0].wait()
    own[1].wait()
    relay(chip, core).start()
    def take_queries(which):
        own[2 + which].wait()
        for step in range(1, chips):
            q_copy(which, step, peer(step)).wait_recv()

    take_queries(0)
    take_queries(1)

    def turn(index):
        return index

    def one_step(index, carry):
        step = turn(index)
        source = peer(step)
        kv_copy(step, source, 0).wait_recv()
        kv_copy(step, source, 1).wait_recv()
        relay(source, core).start()
        done = lax.select(index == 1, chip, peer(turn(index - 1)))
        relay(done, 1 - core).wait_recv()
        attend(done, (0, 1))
        return carry

    lax.fori_loop(1, chips - 2, one_step, 0)
    for step in range(1, chips):
        q_copy(2, step, chip).start()
    lax.fori_loop(chips - 2, chips, one_step, 0)
    last = peer(turn(chips - 1))
    relay(last, 1 - core).wait_recv()

    def o_copy(which, step, head):
        return pltpu.make_async_remote_copy(
            src_ref=held_rows(osend, which, peer(step)),
            dst_ref=head_of(att[which], head),
            send_sem=o_send.at[which, step],
            recv_sem=o_recv.at[which, head],
            device_id=(peer(step) * 2 + core, helper),
            device_id_type=MESH,
        )

    def o_local(which):
        return pltpu.make_async_copy(
            held_rows(osend, which, chip), head_of(att[which], chip), o_own.at[which]
        )

    def give(which):
        for begin, lanes in spans[which]:
            cols = pl.ds(begin, lanes)
            result = acc[:, cols] * (1.0 / total[:, cols])
            osend[cols, :] = result.T.astype(jnp.bfloat16)
        for step in range(1, chips):
            o_copy(which, step, chip).start()
        o_local(which).start()

    def take(which):
        o_local(which).wait()
        for step in range(1, chips):
            o_copy(which, step, peer(step)).wait_recv()

    for which in range(2):
        attend(last, (which,))
        give(which)

    def second_pass(source, carry):
        attend(source, (2,))
        return carry

    wide = w_hbm.shape[1] // parts

    def p_copy(which, index):
        return pltpu.make_async_remote_copy(
            src_ref=psend[which].at[index],
            dst_ref=precv[which].at[index],
            send_sem=p_send.at[which, index],
            recv_sem=p_recv.at[which, index],
            device_id=(ctx, 1 - helper),
            device_id_type=MESH,
        )

    def project_early(which):
        take(which)
        held = pl.ds(which * size[0], size[which])
        for index in range(parts):
            cols = pl.ds(index * wide, wide)
            product = jnp.dot(att[which][...], wbuf[:, cols], preferred_element_type=jnp.float32)
            part[held, cols] = product
            psend[which][index] = product.astype(jnp.bfloat16)
            p_copy(which, index).start()

    w_copy.wait()
    take_queries(2)
    cut = chips // 2
    lax.fori_loop(0, cut, second_pass, 0)
    if cut < chips:
        project_early(0)
        lax.fori_loop(cut, chips, second_pass, 0)
    give(2)
    if cut == chips:
        project_early(0)
    project_early(1)
    take(2)
    spare = swapped - half
    for index in range(parts):
        cols = pl.ds(index * wide, wide)
        product = jnp.dot(att_c[...], wbuf[:, cols], preferred_element_type=jnp.float32)
        part[:half, cols] = jnp.where(
            helper == 0,
            jnp.concatenate([product, part[:spare, cols]], axis=0),
            jnp.concatenate([part[half:, cols], product], axis=0),
        )
    for index in range(parts):
        cols = pl.ds(index * wide, wide)
        for which in range(2):
            p_copy(which, index).wait_recv()
        theirs = jnp.concatenate(
            [precv[i][index].astype(jnp.float32) for i in range(2)], axis=0
        )
        theirs = jnp.where(helper == 0, theirs[:half], theirs[spare:])
        out_ref[:, cols] = (part[:half, cols] + theirs).astype(jnp.bfloat16)

    for step in range(1, chips):
        for which in sets:
            q_copy(which, step, chip).wait_send()
            o_copy(which, step, chip).wait_send()
        for which in range(2):
            kv_copy(step, chip, which).wait_send()
    for source in range(chips):
        relay(source, core).wait_send()
    for which in range(2):
        for index in range(parts):
            p_copy(which, index).wait_send()


def exchanged_body(chips, queries, keys, values, block_pos, w_out):
    rows, width = queries.shape
    out_width = w_out.shape[1]
    count = chips * rows
    parts = 2
    first = -(-(rows // 2) // 16) * 16
    early = 48
    bf16, f32 = jnp.bfloat16, jnp.float32
    dma = pltpu.SemaphoreType.DMA
    anywhere = pl.BlockSpec(memory_space=pltpu.HBM)
    return pl.pallas_call(
        functools.partial(kernel, chips, rows, parts),
        out_shape=jax.ShapeDtypeStruct((rows // 2, out_width), bf16),
        in_specs=[pl.BlockSpec(memory_space=pltpu.SMEM)] + [anywhere] * 4,
        out_specs=pl.BlockSpec(memory_space=pltpu.VMEM),
        scratch_shapes=[
            pltpu.VMEM((count, HEAD_DIM), bf16),
            pltpu.VMEM((chips, 2, 2, rows, HEAD_DIM), bf16),
            pltpu.VMEM((HEAD_DIM, count), f32),
            pltpu.VMEM((1, count), f32),
            pltpu.VMEM((1, count), f32),
            pltpu.VMEM((1, count), jnp.int32),
            pltpu.VMEM((count, HEAD_DIM), bf16),
            pltpu.VMEM((early, width), bf16),
            pltpu.VMEM((first - early, width), bf16),
            pltpu.VMEM((rows - first, width), bf16),
            pltpu.VMEM((width, out_width), bf16),
            pltpu.VMEM((first, out_width), f32),
            pltpu.VMEM((parts, early, out_width // parts), bf16),
            pltpu.VMEM((parts, first - early, out_width // parts), bf16),
            pltpu.VMEM((parts, early, out_width // parts), bf16),
            pltpu.VMEM((parts, first - early, out_width // parts), bf16),
            dma((5,)),
            dma,
            dma((3, chips)),
            dma((3, chips)),
            dma((chips, 2)),
            dma((chips, 2)),
            dma((chips,)),
            dma((chips,)),
            dma((3,)),
            dma((3, chips)),
            dma((3, chips)),
            dma((2, parts)),
            dma((2, parts)),
        ],
        compiler_params=pltpu.CompilerParams(
            collective_id=0, has_side_effects=True, vmem_limit_bytes=60 * 1024 * 1024
        ),
        cost_estimate=pl.CostEstimate(
            flops=8 * count * count * HEAD_DIM + 2 * rows * width * out_width,
            bytes_accessed=2 * (3 * rows * width + width * out_width),
            transcendentals=2 * count * count,
        ),
        name="exchange_attend_project",
    )(block_pos, queries, keys, values, w_out)


def solution(mesh):
    chips = mesh.shape["ctx"] // 2

    def body(queries, keys, values, block_pos, w_out):
        fits = mesh.shape["help"] == 2 and queries.shape[1] == chips * HEAD_DIM
        if fits and chips & (chips - 1) == 0 and queries.shape[0] % 16 == 0:
            return exchanged_body(chips, queries, keys, values, block_pos, w_out)
        return gathered_body(queries, keys, values, block_pos, w_out)

    in_specs = (P("ctx", "help"), P("ctx", "help"), P("ctx", "help"), P(), P("help", None))
    out_specs = P(("ctx", "help"), None)
    return jax.shard_map(body, mesh=mesh, in_specs=in_specs, out_specs=out_specs, check_vma=False)
```
